256 devices in a mesh: row: 16 (over z_hi, y, core), col: 16 (over z_lo, x).
Axes of the slice: x: 4, y: 4, z: 8 (z_hi: 2, z_lo: 4; z = z_hi * 4 + z_lo), core: 2. Of those that a mesh axis runs over, the one named last changes fastest.
Arguments:
- inputs: bfloat16 [512, 9216], P('col', 'row'), may hold values from -6 to 6
- out_grad: bfloat16 [512, 9216], P('col', 'row'), may hold values from -6 to 6
- w_up: bfloat16 [9216, 36864], P('row', 'col'), may hold values from -0.0625 to 0.0625
- w_down: bfloat16 [36864, 9216], P('col', 'row'), may hold values from -0.0625 to 0.0625
Outputs:
- input_grad: bfloat16 [512, 9216], P('col', 'row')
- up_grad: bfloat16 [9216, 36864], P('row', 'col')
- down_grad: bfloat16 [36864, 9216], P('col', 'row')
The draws below stay inside these ranges and needn't reach their ends.
All inputs are finite; a program needn't handle non-finite values.
Results may differ from the reference program's by a relative error of at most 0.0049.
Values may be sent and summed in bfloat16 or wider, within the bound.
A program may use at most 128 MiB of HBM per device.

```python
import jax
import jax.numpy as jnp
from jax import lax

D = 9216
FF = 36864
TOKENS = 512


def strengthened(result, stream_key, source, target, blocks, factor):
    owner, partner = [(jnp.arange(result.shape[dim]) // (result.shape[dim] // blocks)).reshape([-1 if axis == dim else 1 for axis in range(result.ndim)]) for dim in (source, target)]
    chosen = jax.random.permutation(stream_key, blocks)[partner]
    strong = (owner == chosen) | (owner == (partner + blocks // 2) % blocks)
    return jnp.where(strong, factor * result, result)


def levels(rng, extent, shards, least, largest):
    loudness = 1.0
    for position, blocks in shards:
        heights = jax.random.uniform(jax.random.fold_in(jax.random.fold_in(rng, 6), position), (blocks,), jnp.float32, least / len(shards), largest / len(shards))
        loudness = loudness * jnp.repeat(jnp.exp(heights), extent[position] // blocks).reshape((-1,) + (1,) * (len(extent) - 1 - position))
    return loudness


def normal_values(own_key, shape, scale, reach, pieces=(), dtype=jnp.bfloat16):
    gain = levels(own_key, shape, pieces, -0.22, 0.18) if pieces else 1.0
    result = jax.random.normal(own_key, shape, jnp.float32) * scale * gain
    return jnp.minimum(jnp.maximum(result, -reach), reach).astype(dtype)


def noise_with(rng, dims, scale, reach, shards, heavy, held_as=jnp.bfloat16):
    array = scale * jax.random.normal(rng, dims, jnp.float32)
    if shards:
        array = array * levels(rng, dims, shards, -0.22, 0.18)
    return jnp.clip(strengthened(array, jax.random.fold_in(rng, 3), *heavy), -reach, reach).astype(held_as)


def setup_inputs(seed: int = 0) -> dict:
    streams_of = jax.random.split(jax.random.key(seed), 5)
    return {
        "inputs": noise_with(streams_of[0], (TOKENS, D), 1.0, 6.0, ((0, 16), (1, 16)), (1, 0, 16, 2.0)),
        "out_grad": noise_with(streams_of[1], (TOKENS, D), 1.0, 6.0, ((0, 16), (1, 16)), (1, 0, 16, 2.0)),
        "w_up": normal_values(streams_of[2], (D, FF), D ** -0.5, 0.0625, ((0, 16), (1, 16))),
        "w_down": normal_values(streams_of[3], (FF, D), D ** -0.5, 0.0625, ((0, 16), (1, 16))),
    }


def reference(inputs, out_grad, w_up, w_down):
    preact = jnp.dot(inputs, w_up, preferred_element_type=jnp.float32)
    hidden_grad = lax.dot_general(out_grad, w_down, (((1,), (1,)), ((), ())), preferred_element_type=jnp.float32)
    positive = jnp.maximum(preact, 0.0)
    hidden = (positive * positive).astype(jnp.bfloat16)
    preact_grad = (hidden_grad * 2.0 * positive).astype(jnp.bfloat16)
    down_grad = lax.dot_general(hidden, out_grad, (((0,), (0,)), ((), ())), preferred_element_type=jnp.float32).astype(jnp.bfloat16)
    up_grad = lax.dot_general(inputs, preact_grad, (((0,), (0,)), ((), ())), preferred_element_type=jnp.float32).astype(jnp.bfloat16)
    input_grad = lax.dot_general(preact_grad, w_up, (((1,), (1,)), ((), ())), preferred_element_type=jnp.float32).astype(jnp.bfloat16)
    return input_grad, up_grad, down_grad
```

```python
import functools

import jax
import jax.numpy as jnp
from jax import lax
from jax.experimental import pallas as pl
from jax.experimental.pallas import tpu as pltpu
from jax.sharding import PartitionSpec as P

MESH = pl.DeviceIdType.MESH
F32, BF16 = jnp.float32, jnp.bfloat16

PLANES = 4
BLOCK = 32
CHUNK = 128
FEATS = 576
HALF = 1152

ORDER = (
    "U00 U01 C00 P1".split()
    + "P2 C01 P3 R00".split()
    + "U10 R01 U11 C10".split()
    + "U20 Z00 C11 U21".split()
    + "Z01 C20 R10 U30".split()
    + "C21 U31 R11 C30".split()
    + "R20 C31 A00 Z10".split()
    + "R21 Z11 T A01".split()
    + "R30 Z20 R31 A10".split()
    + "H00 F00 Z21 H01".split()
    + "A11 F01 Z30 Z31".split()
    + "A20 F10 H10 E00".split()
    + "F11 A21 H11 E01".split()
    + "I0 F20 H20 A30".split()
    + "E10 E11 I1 A31".split()
    + "H21 F21 E20 H30".split()
    + "J0 F30 F31 H31".split()
    + "J1 E21 E30 I2".split()
    + "E31 I3 G0 J2".split()
    + "J3 G1".split()
)

NAMES = (
    [f"gz{k}" for k in (1, 2, 3)]
    + [f"gx{k}{m}{d}" for k in range(4) for m in range(2) for d in range(3)]
    + [f"{s}{k}{m}" for s in "c r p q z au ad".split() for k in range(4) for m in range(2)]
    + [f"{s}{k}{m}" for s in "ac f fc hc ec".split() for k in range(4) for m in range(2)]
    + [f"ix{k}{d}" for k in range(4) for d in range(3)]
    + [f"iz{k}" for k in (1, 2, 3)]
)
SLOT = {name: i for i, name in enumerate(NAMES)}


def nt(a, b):
    return lax.dot_general(a, b, (((1,), (1,)), ((), ())), preferred_element_type=F32)


def kernel(
    inputs, out_grad, w_up_hbm, w_down_hbm, ig_hbm, up_hbm, down_hbm,
    acts, w_up, w_down, own, give, take, low, r_in, p_in, q_in, total, z_out, z_in, held,
    partial, x_in, iz_out, iz_in, last, x_last, iz_out_last, iz_in_last, ig_out, up_out, down_out, acts_t,
    load_sem, store_sem, send_sem, recv_sem,
):
    row, col = lax.axis_index("row"), lax.axis_index("col")
    z_hi, y, c = row // 8, (row // 2) % 4, row % 2
    z_lo, x = col // 4, col % 4
    oc = 1 - c
    y_up, y_down, y_far = (y + 1) % 4, (y + 3) % 4, (y + 2) % 4
    in_row = lambda h, b, core: (h * 8 + b * 2 + core, col)
    in_col = lambda a, b: (row, a * 4 + b)
    up, down, other, pair = in_row(z_hi, y_up, c), in_row(z_hi, y_down, c), in_row(z_hi, y, oc), in_row(1 - z_hi, y, c)
    xs = [(x + d + 1) % 4 for d in range(3)]
    x_peers = [in_col(z_lo, b) for b in xs]
    flip = [z_lo, 3 - z_lo, (z_lo + 2) % 4, z_lo + 1 - 2 * (z_lo % 2)]
    plane_peers = [in_col(flip[k], x) for k in range(4)]

    weights = (w_up, w_down)
    sends = []

    def remote(name, src, dst, peer):
        i = SLOT[name]
        return pltpu.make_async_remote_copy(
            src_ref=src, dst_ref=dst, send_sem=send_sem.at[i], recv_sem=recv_sem.at[i], device_id=peer, device_id_type=MESH
        )

    def send(name, src, dst, peer):
        copy = remote(name, src, dst, peer)
        copy.start()
        sends.append(copy)

    def arrived(name, dst, peer):
        remote(name, dst, dst, peer).wait_recv()

    loads = [
        pltpu.make_async_copy(inputs, acts.at[0, pl.ds(x * BLOCK, BLOCK)], load_sem.at[0]),
        pltpu.make_async_copy(out_grad, acts.at[1, pl.ds(x * BLOCK, BLOCK)], load_sem.at[1]),
        pltpu.make_async_copy(w_up_hbm, w_up, load_sem.at[2]),
        pltpu.make_async_copy(w_down_hbm, w_down, load_sem.at[3]),
    ]
    for copy in loads:
        copy.start()

    barrier = pltpu.get_barrier_semaphore()
    everyone = [up, down, other, pair] + x_peers + plane_peers[1:]
    for peer in everyone:
        pl.semaphore_signal(barrier, inc=1, device_id=peer, device_id_type=MESH)
    pl.semaphore_wait(barrier, len(everyone))

    def mine(k, b):
        return acts.at[:, pl.ds(k * CHUNK + b * BLOCK, BLOCK)]

    def rows(k, b):
        return pl.ds(k * CHUNK + b * BLOCK, BLOCK)

    def block(b):
        return pl.ds(pl.multiple_of(b * BLOCK, BLOCK), BLOCK)

    def mine1(k, m, b):
        return acts.at[m, pl.ds(k * CHUNK + b * BLOCK, BLOCK)]

    def along_x(k, m):
        for d in (1, 0, 2):
            send(f"gx{k}{m}{d}", mine1(k, m, x), mine1(k, m, x), x_peers[d])

    for m in range(2):
        loads[m].wait()
        along_x(0, m)
    for k in (1, 2, 3):
        send(f"gz{k}", mine(0, x), mine(k, x), plane_peers[k])

    def P(k):
        arrived(f"gz{k}", mine(k, x), plane_peers[k])
        for m in range(2):
            along_x(k, m)

    def U(k, m):
        for d in range(3):
            arrived(f"gx{k}{m}{d}", mine1(k, m, xs[2 - d]), x_peers[d])
        if k == 0:
            loads[2 + m].wait()
        a = acts[m, k * CHUNK : (k + 1) * CHUNK, :]
        for half, into in ((oc, give), (c, own)):
            at = pl.ds(pl.multiple_of(half * HALF, 128), HALF)
            into[k, m] = jnp.dot(a, weights[m][:, at], preferred_element_type=F32)
            if into is give:
                send(f"c{k}{m}", give.at[k, m], take.at[k, m], other)

    def both(k, m, b):
        return own[k, m, block(b), :] + take[k, m, block(b), :]

    def C(k, m):
        arrived(f"c{k}{m}", take.at[k, m], other)
        far_peer, near_name, near, near_peer, near_in = ((up, "q", y_down, down, q_in), (down, "p", y_up, up, p_in))[m]
        low[k, m, block(y_far), :] = both(k, m, y_far).astype(BF16)
        send(f"r{k}{m}", low.at[k, m, block(y_far)], r_in.at[k, m], far_peer)
        low[k, m, block(near), :] = both(k, m, near).astype(BF16)
        send(f"{near_name}{k}{m}", low.at[k, m, block(near)], near_in.at[k, m], near_peer)

    def R(k, m):
        source, name, to, peer, into = ((down, "p", y_up, up, p_in), (up, "q", y_down, down, q_in))[m]
        arrived(f"r{k}{m}", r_in.at[k, m], source)
        low[k, m, block(to), :] = (both(k, m, to) + r_in[k, m].astype(F32)).astype(BF16)
        send(f"{name}{k}{m}", low.at[k, m, block(to)], into.at[k, m], peer)

    def Z(k, m):
        arrived(f"p{k}{m}", p_in.at[k, m], down)
        arrived(f"q{k}{m}", q_in.at[k, m], up)
        summed = both(k, m, y) + p_in[k, m].astype(F32) + q_in[k, m].astype(F32)
        total[k, m] = summed
        z_out[k, m] = summed.astype(BF16)
        send(f"z{k}{m}", z_out.at[k, m], z_in.at[k, m], pair)

    def A(k, m):
        arrived(f"z{k}{m}", z_in.at[k, m], pair)
        positive = jnp.maximum(total[k, 0] + z_in[k, 0].astype(F32), 0.0)
        if m == 0:
            held[0, c, rows(k, y), :] = (positive * positive).astype(BF16)
        else:
            hidden_grad = total[k, 1] + z_in[k, 1].astype(F32)
            held[1, c, rows(k, y), :] = (hidden_grad * 2.0 * positive).astype(BF16)
        here = held.at[m, c, rows(k, y)]
        send(f"au{k}{m}", here, here, up)
        send(f"ad{k}{m}", here, here, down)
        send(f"ac{k}{m}", here, here, other)

    def F(k, m):
        name, b, source, peer = (("au", y_down, down, up), ("ad", y_up, up, down))[m]
        there = held.at[m, c, rows(k, b)]
        arrived(f"{name}{k}{m}", there, source)
        send(f"f{k}{m}", there, there, peer)
        send(f"fc{k}{m}", there, there, other)

    def H(k, m):
        name, b, source = (("ad", y_up, up), ("au", y_down, down))[m]
        there = held.at[m, c, rows(k, b)]
        arrived(f"{name}{k}{m}", there, source)
        send(f"hc{k}{m}", there, there, other)

    def E(k, m):
        far = held.at[m, c, rows(k, y_far)]
        arrived(f"f{k}{m}", far, (down, up)[m])
        send(f"ec{k}{m}", far, far, other)

    def whole(k, m):
        arrived(f"ac{k}{m}", held.at[m, oc, rows(k, y)], other)
        arrived(f"fc{k}{m}", held.at[m, oc, rows(k, (y_down, y_up)[m])], other)
        arrived(f"hc{k}{m}", held.at[m, oc, rows(k, (y_up, y_down)[m])], other)
        arrived(f"ec{k}{m}", held.at[m, oc, rows(k, y_far)], other)

    def I(k):
        whole(k, 1)
        at = slice(k * CHUNK, (k + 1) * CHUNK)
        partial[k] = nt(held[1, 0, at, :], w_up[:, :HALF]) + nt(held[1, 1, at, :], w_up[:, HALF:])
        if k == 3:
            last[...] = partial[k].astype(BF16)
        for d in (1, 0, 2):
            if k == 3:
                send(f"ix{k}{d}", last.at[block(xs[d])], x_last.at[d], x_peers[d])
            else:
                send(f"ix{k}{d}", partial.at[k, block(xs[d])], x_in.at[k, d], x_peers[d])

    def J(k):
        landed = x_last if k == 3 else x_in.at[k]
        for d in range(3):
            arrived(f"ix{k}{d}", landed.at[d], x_peers[d])
        summed = partial[k, block(x), :]
        for d in range(3):
            summed = summed + landed[d].astype(F32)
        if k == 0:
            partial[k, block(x), :] = summed
        elif k == 3:
            iz_out_last[...] = summed.astype(BF16)
            send(f"iz{k}", iz_out_last, iz_in_last, plane_peers[k])
        else:
            iz_out[k - 1] = summed
            send(f"iz{k}", iz_out.at[k - 1], iz_in.at[k - 1], plane_peers[k])

    stores = []

    def store(src, dst):
        copy = pltpu.make_async_copy(src, dst, store_sem.at[len(stores)])
        copy.start()
        stores.append(copy)

    def T():
        for m in range(2):
            acts_t[m] = acts[m].T

    def G(m):
        out, dst = ((down_out, down_hbm), (up_out, up_hbm))[m]
        if m == 0:
            for k in range(4):
                whole(k, 0)
        for h in range(2):
            at = pl.ds(h * HALF, HALF)
            out[:, at] = jnp.dot(acts_t[1 - m], held[m, h], preferred_element_type=F32).astype(BF16)
            store(out.at[:, at], dst.at[:, at])

    stages = dict(P=P, U=U, C=C, R=R, Z=Z, A=A, F=F, H=H, E=E, I=I, J=J, T=T, G=G)
    for item in ORDER:
        stages[item[0]](*map(int, item[1:]))

    summed = partial[0, block(x), :]
    for k in (1, 2):
        arrived(f"iz{k}", iz_in.at[k - 1], plane_peers[k])
        summed = summed + iz_in[k - 1]
    arrived("iz3", iz_in_last, plane_peers[3])
    summed = summed + iz_in_last[...].astype(F32)
    ig_out[...] = summed.astype(BF16)
    store(ig_out, ig_hbm)
    for copy in sends:
        copy.wait_send()
    for copy in stores:
        copy.wait()


def shards(inputs, out_grad, w_up, w_down):
    anywhere = pl.BlockSpec(memory_space=pl.ANY)
    n = len(NAMES)
    input_grad, up_grad, down_grad_t = pl.pallas_call(
        kernel,
        out_shape=(
            jax.ShapeDtypeStruct((BLOCK, FEATS), BF16),
            jax.ShapeDtypeStruct((FEATS, 2 * HALF), BF16),
            jax.ShapeDtypeStruct((FEATS, 2 * HALF), BF16),
        ),
        in_specs=[anywhere] * 4,
        out_specs=(anywhere,) * 3,
        scratch_shapes=[
            pltpu.VMEM((2, PLANES * CHUNK, FEATS), BF16),
            pltpu.VMEM((FEATS, 2 * HALF), BF16),
            pltpu.VMEM((FEATS, 2 * HALF), BF16),
            pltpu.VMEM((PLANES, 2, CHUNK, HALF), F32),
            pltpu.VMEM((PLANES, 2, CHUNK, HALF), F32),
            pltpu.VMEM((PLANES, 2, CHUNK, HALF), F32),
            pltpu.VMEM((PLANES, 2, CHUNK, HALF), BF16),
            pltpu.VMEM((PLANES, 2, BLOCK, HALF), BF16),
            pltpu.VMEM((PLANES, 2, BLOCK, HALF), BF16),
            pltpu.VMEM((PLANES, 2, BLOCK, HALF), BF16),
            pltpu.VMEM((PLANES, 2, BLOCK, HALF), F32),
            pltpu.VMEM((PLANES, 2, BLOCK, HALF), BF16),
            pltpu.VMEM((PLANES, 2, BLOCK, HALF), BF16),
            pltpu.VMEM((2, 2, PLANES * CHUNK, HALF), BF16),
            pltpu.VMEM((PLANES, CHUNK, FEATS), F32),
            pltpu.VMEM((3, 3, BLOCK, FEATS), F32),
            pltpu.VMEM((2, BLOCK, FEATS), F32),
            pltpu.VMEM((2, BLOCK, FEATS), F32),
            pltpu.VMEM((CHUNK, FEATS), BF16),
            pltpu.VMEM((3, BLOCK, FEATS), BF16),
            pltpu.VMEM((BLOCK, FEATS), BF16),
            pltpu.VMEM((BLOCK, FEATS), BF16),
            pltpu.VMEM((BLOCK, FEATS), BF16),
            pltpu.VMEM((FEATS, 2 * HALF), BF16),
            pltpu.VMEM((FEATS, 2 * HALF), BF16),
            pltpu.VMEM((2, FEATS, PLANES * CHUNK), BF16),
            pltpu.SemaphoreType.DMA((4,)),
            pltpu.SemaphoreType.DMA((5,)),
            pltpu.SemaphoreType.DMA((n,)),
            pltpu.SemaphoreType.DMA((n,)),
        ],
        compiler_params=pltpu.CompilerParams(collective_id=0, has_side_effects=True, vmem_limit_bytes=60 * 2**20),
        cost_estimate=pl.CostEstimate(flops=6_800_000_000, bytes_accessed=11_000_000, transcendentals=0),
        name="ffn_backward",
    )(inputs, out_grad, w_up, w_down.T)
    return input_grad, up_grad, down_grad_t.T


def solution(mesh):
    in_specs = (P("col", "row"), P("col", "row"), P("row", "col"), P("col", "row"))
    out_specs = (P("col", "row"), P("row", "col"), P("col", "row"))
    return jax.shard_map(shards, mesh=mesh, in_specs=in_specs, out_specs=out_specs, check_vma=False)
```

```python
import functools

import jax
import jax.numpy as jnp
from jax import lax
from jax.experimental import pallas as pl
from jax.experimental.pallas import tpu as pltpu
from jax.sharding import PartitionSpec as P

MESH = pl.DeviceIdType.MESH
F32, BF16 = jnp.float32, jnp.bfloat16

PLANES = 4
BLOCK = 32
CHUNK = 128
FEATS = 576
HALF = 1152

ORDER = (
    "P1 U00 P2 U01".split()
    + "C00 U10 C01 U11".split()
    + "R00 P3 C10 U20".split()
    + "R01 C11 C20 U21".split()
    + "Z00 R10 Z01 C21".split()
    + "U30 U31 R11 R20".split()
    + "Z10 C31 R21 C30".split()
    + "Z11 R31 Z20 A00".split()
    + "R30 A01 Z21 Z31".split()
    + "A11 A10 F01 Z30".split()
    + "F11 H01 A21 A20".split()
    + "E01 F10 E11 A31".split()
    + "H11 I0 F21 H20".split()
    + "I1 H21 T H10".split()
    + "F31 H31 E21 A30".split()
    + "F20 I2 F00 E31".split()
    + "E10 F30 I3 H30".split()
    + "H00 J1 G1 J2".split()
    + "E20 E00 J0 E30".split()
    + "J3 G0".split()
)


NAMES = (
    [f"gz{k}" for k in (1, 2, 3)]
    + [f"gx{k}{m}{d}" for k in range(4) for m in range(2) for d in range(3)]
    + [f"{s}{k}{m}" for s in ("c", "r", "p", "q", "z", "au", "ad") for k in range(4) for m in range(2)]
    + [f"{s}{k}{m}" for s in ("ac", "f", "fc", "hc", "ec") for k in range(4) for m in range(2)]
    + [f"ix{k}{d}" for k in range(4) for d in range(3)]
    + [f"iz{k}" for k in (1, 2, 3)]
)
SLOT = {name: i for i, name in enumerate(NAMES)}


def nt(a, b):
    return lax.dot_general(a, b, (((1,), (1,)), ((), ())), preferred_element_type=F32)


def kernel(
    inputs, out_grad, w_up_hbm, w_down_hbm, ig_hbm, up_hbm, down_hbm,
    acts, w_up, w_down, own, give, take, low, r_in, p_in, q_in, total, z_out, z_in, held,
    partial, x_in, iz_out, iz_in, last, x_last, iz_out_last, iz_in_last, ig_out, up_out, down_out, acts_t,
    load_sem, store_sem, send_sem, recv_sem,
):
    row, col = lax.axis_index("row"), lax.axis_index("col")
    z_hi, y, c = row // 8, (row // 2) % 4, row % 2
    z_lo, x = col // 4, col % 4
    oc = 1 - c
    y_up, y_down, y_far = (y + 1) % 4, (y + 3) % 4, (y + 2) % 4
    in_row = lambda h, b, core: (h * 8 + b * 2 + core, col)
    in_col = lambda a, b: (row, a * 4 + b)
    up, down, other, pair = in_row(z_hi, y_up, c), in_row(z_hi, y_down, c), in_row(z_hi, y, oc), in_row(1 - z_hi, y, c)
    xs = [(x + d + 1) % 4 for d in range(3)]
    x_peers = [in_col(z_lo, b) for b in xs]
    flip = [z_lo, 3 - z_lo, (z_lo + 2) % 4, z_lo + 1 - 2 * (z_lo % 2)]
    plane_peers = [in_col(flip[k], x) for k in range(4)]

    weights = (w_up, w_down)
    sends, seen = [], set()

    def remote(name, src, dst, peer):
        i = SLOT[name]
        return pltpu.make_async_remote_copy(
            src_ref=src, dst_ref=dst, send_sem=send_sem.at[i], recv_sem=recv_sem.at[i], device_id=peer, device_id_type=MESH
        )

    def send(name, src, dst, peer):
        copy = remote(name, src, dst, peer)
        copy.start()
        sends.append(copy)

    def arrived(name, dst, peer):
        if name in seen:
            return
        seen.add(name)
        remote(name, dst, dst, peer).wait_recv()

    loads = [
        pltpu.make_async_copy(inputs, acts.at[0, pl.ds(x * BLOCK, BLOCK)], load_sem.at[0]),
        pltpu.make_async_copy(out_grad, acts.at[1, pl.ds(x * BLOCK, BLOCK)], load_sem.at[1]),
        pltpu.make_async_copy(w_up_hbm, w_up, load_sem.at[2]),
        pltpu.make_async_copy(w_down_hbm, w_down, load_sem.at[3]),
    ]
    for copy in loads:
        copy.start()

    barrier = pltpu.get_barrier_semaphore()
    everyone = [up, down, other, pair] + x_peers + plane_peers[1:]
    for peer in everyone:
        pl.semaphore_signal(barrier, inc=1, device_id=peer, device_id_type=MESH)
    pl.semaphore_wait(barrier, len(everyone))

    def mine(k, b):
        return acts.at[:, pl.ds(k * CHUNK + b * BLOCK, BLOCK)]

    def rows(k, b):
        return pl.ds(k * CHUNK + b * BLOCK, BLOCK)

    def block(b):
        return pl.ds(pl.multiple_of(b * BLOCK, BLOCK), BLOCK)

    def mine1(k, m, b):
        return acts.at[m, pl.ds(k * CHUNK + b * BLOCK, BLOCK)]

    def along_x(k, m):
        for d in (1, 0, 2):
            send(f"gx{k}{m}{d}", mine1(k, m, x), mine1(k, m, x), x_peers[d])

    for m in range(2):
        loads[m].wait()
        along_x(0, m)
    for k in (1, 2, 3):
        send(f"gz{k}", mine(0, x), mine(k, x), plane_peers[k])

    def P(k):
        arrived(f"gz{k}", mine(k, x), plane_peers[k])
        for m in range(2):
            along_x(k, m)

    def U(k, m):
        for d in range(3):
            arrived(f"gx{k}{m}{d}", mine1(k, m, xs[2 - d]), x_peers[d])
        if k == 0:
            loads[2 + m].wait()
        a = acts[m, k * CHUNK : (k + 1) * CHUNK, :]
        for half, into in ((oc, give), (c, own)):
            at = pl.ds(pl.multiple_of(half * HALF, 128), HALF)
            into[k, m] = jnp.dot(a, weights[m][:, at], preferred_element_type=F32)
            if into is give:
                send(f"c{k}{m}", give.at[k, m], take.at[k, m], other)

    def both(k, m, b):
        return own[k, m, block(b), :] + take[k, m, block(b), :]

    def C(k, m):
        arrived(f"c{k}{m}", take.at[k, m], other)
        far_peer, near_name, near, near_peer, near_in = ((up, "q", y_down, down, q_in), (down, "p", y_up, up, p_in))[m]
        low[k, m, block(y_far), :] = both(k, m, y_far).astype(BF16)
        send(f"r{k}{m}", low.at[k, m, block(y_far)], r_in.at[k, m], far_peer)
        low[k, m, block(near), :] = both(k, m, near).astype(BF16)
        send(f"{near_name}{k}{m}", low.at[k, m, block(near)], near_in.at[k, m], near_peer)

    def R(k, m):
        source, name, to, peer, into = ((down, "p", y_up, up, p_in), (up, "q", y_down, down, q_in))[m]
        arrived(f"r{k}{m}", r_in.at[k, m], source)
        low[k, m, block(to), :] = (both(k, m, to) + r_in[k, m].astype(F32)).astype(BF16)
        send(f"{name}{k}{m}", low.at[k, m, block(to)], into.at[k, m], peer)

    def Z(k, m):
        arrived(f"p{k}{m}", p_in.at[k, m], down)
        arrived(f"q{k}{m}", q_in.at[k, m], up)
        summed = both(k, m, y) + p_in[k, m].astype(F32) + q_in[k, m].astype(F32)
        total[k, m] = summed
        z_out[k, m] = summed.astype(BF16)
        send(f"z{k}{m}", z_out.at[k, m], z_in.at[k, m], pair)

    def A(k, m):
        for p in range(m + 1):
            arrived(f"z{k}{p}", z_in.at[k, p], pair)
        positive = jnp.maximum(total[k, 0] + z_in[k, 0].astype(F32), 0.0)
        if m == 0:
            held[0, c, rows(k, y), :] = (positive * positive).astype(BF16)
        else:
            hidden_grad = total[k, 1] + z_in[k, 1].astype(F32)
            held[1, c, rows(k, y), :] = (hidden_grad * 2.0 * positive).astype(BF16)
        here = held.at[m, c, rows(k, y)]
        send(f"au{k}{m}", here, here, up)
        send(f"ad{k}{m}", here, here, down)
        send(f"ac{k}{m}", here, here, other)

    def F(k, m):
        name, b, source, peer = (("au", y_down, down, up), ("ad", y_up, up, down))[m]
        there = held.at[m, c, rows(k, b)]
        arrived(f"{name}{k}{m}", there, source)
        send(f"f{k}{m}", there, there, peer)
        send(f"fc{k}{m}", there, there, other)

    def H(k, m):
        name, b, source = (("ad", y_up, up), ("au", y_down, down))[m]
        there = held.at[m, c, rows(k, b)]
        arrived(f"{name}{k}{m}", there, source)
        send(f"hc{k}{m}", there, there, other)

    def E(k, m):
        far = held.at[m, c, rows(k, y_far)]
        arrived(f"f{k}{m}", far, (down, up)[m])
        send(f"ec{k}{m}", far, far, other)

    def whole(k, m):
        arrived(f"ac{k}{m}", held.at[m, oc, rows(k, y)], other)
        arrived(f"fc{k}{m}", held.at[m, oc, rows(k, (y_down, y_up)[m])], other)
        arrived(f"hc{k}{m}", held.at[m, oc, rows(k, (y_up, y_down)[m])], other)
        arrived(f"ec{k}{m}", held.at[m, oc, rows(k, y_far)], other)

    def I(k):
        whole(k, 1)
        at = slice(k * CHUNK, (k + 1) * CHUNK)
        partial[k] = nt(held[1, 0, at, :], w_up[:, :HALF]) + nt(held[1, 1, at, :], w_up[:, HALF:])
        if k == 3:
            last[...] = partial[k].astype(BF16)
        for d in (1, 0, 2):
            if k == 3:
                send(f"ix{k}{d}", last.at[block(xs[d])], x_last.at[d], x_peers[d])
            else:
                send(f"ix{k}{d}", partial.at[k, block(xs[d])], x_in.at[k, d], x_peers[d])

    def J(k):
        landed = x_last if k == 3 else x_in.at[k]
        for d in range(3):
            arrived(f"ix{k}{d}", landed.at[d], x_peers[d])
        summed = partial[k, block(x), :]
        for d in range(3):
            summed = summed + landed[d].astype(F32)
        if k == 0:
            partial[k, block(x), :] = summed
        elif k == 3:
            iz_out_last[...] = summed.astype(BF16)
            send(f"iz{k}", iz_out_last, iz_in_last, plane_peers[k])
        else:
            iz_out[k - 1] = summed
            send(f"iz{k}", iz_out.at[k - 1], iz_in.at[k - 1], plane_peers[k])

    stores = []

    def store(src, dst):
        copy = pltpu.make_async_copy(src, dst, store_sem.at[len(stores)])
        copy.start()
        stores.append(copy)

    def T():
        for m in range(2):
            acts_t[m] = acts[m].T

    def G(m):
        out, dst = ((down_out, down_hbm), (up_out, up_hbm))[m]
        if m == 0:
            for k in range(4):
                whole(k, 0)
        for h in range(2):
            at = pl.ds(h * HALF, HALF)
            out[:, at] = jnp.dot(acts_t[1 - m], held[m, h], preferred_element_type=F32).astype(BF16)
            store(out.at[:, at], dst.at[:, at])

    stages = dict(P=P, U=U, C=C, R=R, Z=Z, A=A, F=F, H=H, E=E, I=I, J=J, T=T, G=G)
    for item in ORDER:
        stages[item[0]](*map(int, item[1:]))

    summed = partial[0, block(x), :]
    for k in (1, 2):
        arrived(f"iz{k}", iz_in.at[k - 1], plane_peers[k])
        summed = summed + iz_in[k - 1]
    arrived("iz3", iz_in_last, plane_peers[3])
    summed = summed + iz_in_last[...].astype(F32)
    ig_out[...] = summed.astype(BF16)
    store(ig_out, ig_hbm)
    for copy in sends:
        copy.wait_send()
    for copy in stores:
        copy.wait()


def hand_over(ig, up, down, ig_to, up_to, down_to, sem):
    copies = [pltpu.make_async_copy(ig, ig_to, sem.at[8])]
    for i in range(4):
        at = pl.ds(i * 144, 144)
        copies.append(pltpu.make_async_copy(up.at[at], up_to.at[at], sem.at[i]))
        copies.append(pltpu.make_async_copy(down.at[at], down_to.at[at], sem.at[4 + i]))
    for copy in copies:
        copy.start()
    for copy in copies:
        copy.wait()


def shards(inputs, out_grad, w_up, w_down):
    anywhere = pl.BlockSpec(memory_space=pl.ANY)
    n = len(NAMES)
    input_grad, up_grad, down_grad_t = pl.pallas_call(
        kernel,
        out_shape=(
            jax.ShapeDtypeStruct((BLOCK, FEATS), BF16),
            jax.ShapeDtypeStruct((FEATS, 2 * HALF), BF16),
            jax.ShapeDtypeStruct((FEATS, 2 * HALF), BF16),
        ),
        in_specs=[pl.BlockSpec(memory_space=pltpu.HBM)] * 4,
        out_specs=(anywhere,) * 3,
        scratch_shapes=[
            pltpu.VMEM((2, PLANES * CHUNK, FEATS), BF16),
            pltpu.VMEM((FEATS, 2 * HALF), BF16),
            pltpu.VMEM((FEATS, 2 * HALF), BF16),
            pltpu.VMEM((PLANES, 2, CHUNK, HALF), F32),
            pltpu.VMEM((PLANES, 2, CHUNK, HALF), F32),
            pltpu.VMEM((PLANES, 2, CHUNK, HALF), F32),
            pltpu.VMEM((PLANES, 2, CHUNK, HALF), BF16),
            pltpu.VMEM((PLANES, 2, BLOCK, HALF), BF16),
            pltpu.VMEM((PLANES, 2, BLOCK, HALF), BF16),
            pltpu.VMEM((PLANES, 2, BLOCK, HALF), BF16),
            pltpu.VMEM((PLANES, 2, BLOCK, HALF), F32),
            pltpu.VMEM((PLANES, 2, BLOCK, HALF), BF16),
            pltpu.VMEM((PLANES, 2, BLOCK, HALF), BF16),
            pltpu.VMEM((2, 2, PLANES * CHUNK, HALF), BF16),
            pltpu.VMEM((PLANES, CHUNK, FEATS), F32),
            pltpu.VMEM((3, 3, BLOCK, FEATS), F32),
            pltpu.VMEM((2, BLOCK, FEATS), F32),
            pltpu.VMEM((2, BLOCK, FEATS), F32),
            pltpu.VMEM((CHUNK, FEATS), BF16),
            pltpu.VMEM((3, BLOCK, FEATS), BF16),
            pltpu.VMEM((BLOCK, FEATS), BF16),
            pltpu.VMEM((BLOCK, FEATS), BF16),
            pltpu.VMEM((BLOCK, FEATS), BF16),
            pltpu.VMEM((FEATS, 2 * HALF), BF16),
            pltpu.VMEM((FEATS, 2 * HALF), BF16),
            pltpu.VMEM((2, FEATS, PLANES * CHUNK), BF16),
            pltpu.SemaphoreType.DMA((4,)),
            pltpu.SemaphoreType.DMA((5,)),
            pltpu.SemaphoreType.DMA((n,)),
            pltpu.SemaphoreType.DMA((n,)),
        ],
        compiler_params=pltpu.CompilerParams(collective_id=0, has_side_effects=True, vmem_limit_bytes=46 * 2**20),
        cost_estimate=pl.CostEstimate(flops=6_800_000_000, bytes_accessed=11_000_000, transcendentals=0),
        name="ffn_backward",
    )(*(pltpu.with_memory_space_constraint(a, pltpu.HBM) for a in (inputs, out_grad, w_up, w_down.T)))
    input_grad, up_grad, down_grad_t = pl.pallas_call(
        hand_over,
        out_shape=tuple(jax.ShapeDtypeStruct(a.shape, a.dtype) for a in (input_grad, up_grad, down_grad_t)),
        in_specs=[anywhere] * 3,
        out_specs=(anywhere,) * 3,
        scratch_shapes=[pltpu.SemaphoreType.DMA((9,))],
        compiler_params=pltpu.CompilerParams(vmem_limit_bytes=2 * 2**20),
        cost_estimate=pl.CostEstimate(flops=0, bytes_accessed=10_700_000, transcendentals=0),
        name="hand_over",
    )(input_grad, up_grad, down_grad_t)
    return input_grad, up_grad, down_grad_t.T


def solution(mesh):
    in_specs = (P("col", "row"), P("col", "row"), P("row", "col"), P("col", "row"))
    out_specs = (P("col", "row"), P("row", "col"), P("col", "row"))
    return jax.shard_map(shards, mesh=mesh, in_specs=in_specs, out_specs=out_specs, check_vma=False)
```

```python
import functools

import jax
import jax.numpy as jnp
from jax import lax
from jax.experimental import pallas as pl
from jax.experimental.pallas import tpu as pltpu
from jax.sharding import PartitionSpec as P

MESH = pl.DeviceIdType.MESH
F32, BF16 = jnp.float32, jnp.bfloat16

PLANES = 4
BLOCK = 32
CHUNK = 128
FEATS = 576
HALF = 1152

ORDER = (
    "P1 U00 P2 U01".split()
    + "C00 U10 C01 U11".split()
    + "R00 P3 C10 U20".split()
    + "R01 C11 C20 U21".split()
    + "Z00 R10 Z01 C21".split()
    + "U30 U31 R11 R20".split()
    + "Z10 C31 R21 C30".split()
    + "Z11 R31 Z20 A00".split()
    + "R30 A01 Z21 Z31".split()
    + "A11 A10 F01 Z30".split()
    + "F11 H01 A21 A20".split()
    + "E01 F10 E11 A31".split()
    + "H11 I0 F21 H20".split()
    + "I1 H21 T H10".split()
    + "F31 H31 E21 A30".split()
    + "F20 I2 F00 E31".split()
    + "E10 F30 I3 H30".split()
    + "H00 J1 G1 J2".split()
    + "E20 E00 J0 E30".split()
    + "J3 G0".split()
)


NAMES = (
    [f"gz{k}" for k in (1, 2, 3)]
    + [f"gx{k}{m}{d}" for k in range(4) for m in range(2) for d in range(3)]
    + [f"{s}{k}{m}" for s in ("c", "r", "p", "q", "z", "au", "ad") for k in range(4) for m in range(2)]
    + [f"{s}{k}{m}" for s in ("ac", "f", "fc", "hc", "ec") for k in range(4) for m in range(2)]
    + [f"ix{k}{d}" for k in range(4) for d in range(3)]
    + [f"iz{k}" for k in (1, 2, 3)]
)
SLOT = {name: i for i, name in enumerate(NAMES)}


def nt(a, b):
    return lax.dot_general(a, b, (((1,), (1,)), ((), ())), preferred_element_type=F32)


def kernel(
    inputs, out_grad, w_up_hbm, w_down_hbm, ig_hbm, up_out, down_out,
    acts, w_up, w_down, own, give, take, low, r_in, p_in, q_in, total, z_out, z_in, held,
    partial, x_in, iz_out, iz_in, last, x_last, iz_out_last, iz_in_last, ig_out, acts_t,
    load_sem, store_sem, send_sem, recv_sem,
):
    row, col = lax.axis_index("row"), lax.axis_index("col")
    z_hi, y, c = row // 8, (row // 2) % 4, row % 2
    z_lo, x = col // 4, col % 4
    oc = 1 - c
    y_up, y_down, y_far = (y + 1) % 4, (y + 3) % 4, (y + 2) % 4
    in_row = lambda h, b, core: (h * 8 + b * 2 + core, col)
    in_col = lambda a, b: (row, a * 4 + b)
    up, down, other, pair = in_row(z_hi, y_up, c), in_row(z_hi, y_down, c), in_row(z_hi, y, oc), in_row(1 - z_hi, y, c)
    xs = [(x + d + 1) % 4 for d in range(3)]
    x_peers = [in_col(z_lo, b) for b in xs]
    flip = [z_lo, 3 - z_lo, (z_lo + 2) % 4, z_lo + 1 - 2 * (z_lo % 2)]
    plane_peers = [in_col(flip[k], x) for k in range(4)]

    weights = (w_up, w_down)
    sends, seen = [], set()

    def remote(name, src, dst, peer):
        i = SLOT[name]
        return pltpu.make_async_remote_copy(
            src_ref=src, dst_ref=dst, send_sem=send_sem.at[i], recv_sem=recv_sem.at[i], device_id=peer, device_id_type=MESH
        )

    def send(name, src, dst, peer):
        copy = remote(name, src, dst, peer)
        copy.start()
        sends.append(copy)

    def arrived(name, dst, peer):
        if name in seen:
            return
        seen.add(name)
        remote(name, dst, dst, peer).wait_recv()

    loads = [
        pltpu.make_async_copy(inputs, acts.at[0, pl.ds(x * BLOCK, BLOCK)], load_sem.at[0]),
        pltpu.make_async_copy(out_grad, acts.at[1, pl.ds(x * BLOCK, BLOCK)], load_sem.at[1]),
        pltpu.make_async_copy(w_up_hbm, w_up, load_sem.at[2]),
        pltpu.make_async_copy(w_down_hbm, w_down, load_sem.at[3]),
    ]
    for copy in loads:
        copy.start()

    barrier = pltpu.get_barrier_semaphore()
    everyone = [up, down, other, pair] + x_peers + plane_peers[1:]
    for peer in everyone:
        pl.semaphore_signal(barrier, inc=1, device_id=peer, device_id_type=MESH)
    pl.semaphore_wait(barrier, len(everyone))

    def mine(k, b):
        return acts.at[:, pl.ds(k * CHUNK + b * BLOCK, BLOCK)]

    def rows(k, b):
        return pl.ds(k * CHUNK + b * BLOCK, BLOCK)

    def block(b):
        return pl.ds(pl.multiple_of(b * BLOCK, BLOCK), BLOCK)

    def mine1(k, m, b):
        return acts.at[m, pl.ds(k * CHUNK + b * BLOCK, BLOCK)]

    def along_x(k, m):
        for d in (1, 0, 2):
            send(f"gx{k}{m}{d}", mine1(k, m, x), mine1(k, m, x), x_peers[d])

    for m in range(2):
        loads[m].wait()
        along_x(0, m)
    for k in (1, 2, 3):
        send(f"gz{k}", mine(0, x), mine(k, x), plane_peers[k])

    def P(k):
        arrived(f"gz{k}", mine(k, x), plane_peers[k])
        for m in range(2):
            along_x(k, m)

    def U(k, m):
        for d in range(3):
            arrived(f"gx{k}{m}{d}", mine1(k, m, xs[2 - d]), x_peers[d])
        if k == 0:
            loads[2 + m].wait()
        a = acts[m, k * CHUNK : (k + 1) * CHUNK, :]
        for half, into in ((oc, give), (c, own)):
            at = pl.ds(pl.multiple_of(half * HALF, 128), HALF)
            into[k, m] = jnp.dot(a, weights[m][:, at], preferred_element_type=F32)
            if into is give:
                send(f"c{k}{m}", give.at[k, m], take.at[k, m], other)

    def both(k, m, b):
        return own[k, m, block(b), :] + take[k, m, block(b), :]

    def C(k, m):
        arrived(f"c{k}{m}", take.at[k, m], other)
        far_peer, near_name, near, near_peer, near_in = ((up, "q", y_down, down, q_in), (down, "p", y_up, up, p_in))[m]
        low[k, m, block(y_far), :] = both(k, m, y_far).astype(BF16)
        send(f"r{k}{m}", low.at[k, m, block(y_far)], r_in.at[k, m], far_peer)
        low[k, m, block(near), :] = both(k, m, near).astype(BF16)
        send(f"{near_name}{k}{m}", low.at[k, m, block(near)], near_in.at[k, m], near_peer)

    def R(k, m):
        source, name, to, peer, into = ((down, "p", y_up, up, p_in), (up, "q", y_down, down, q_in))[m]
        arrived(f"r{k}{m}", r_in.at[k, m], source)
        low[k, m, block(to), :] = (both(k, m, to) + r_in[k, m].astype(F32)).astype(BF16)
        send(f"{name}{k}{m}", low.at[k, m, block(to)], into.at[k, m], peer)

    def Z(k, m):
        arrived(f"p{k}{m}", p_in.at[k, m], down)
        arrived(f"q{k}{m}", q_in.at[k, m], up)
        summed = both(k, m, y) + p_in[k, m].astype(F32) + q_in[k, m].astype(F32)
        total[k, m] = summed
        z_out[k, m] = summed.astype(BF16)
        send(f"z{k}{m}", z_out.at[k, m], z_in.at[k, m], pair)

    def A(k, m):
        for p in range(m + 1):
            arrived(f"z{k}{p}", z_in.at[k, p], pair)
        positive = jnp.maximum(total[k, 0] + z_in[k, 0].astype(F32), 0.0)
        if m == 0:
            held[0, c, rows(k, y), :] = (positive * positive).astype(BF16)
        else:
            hidden_grad = total[k, 1] + z_in[k, 1].astype(F32)
            held[1, c, rows(k, y), :] = (hidden_grad * 2.0 * positive).astype(BF16)
        here = held.at[m, c, rows(k, y)]
        send(f"au{k}{m}", here, here, up)
        send(f"ad{k}{m}", here, here, down)
        send(f"ac{k}{m}", here, here, other)

    def F(k, m):
        name, b, source, peer = (("au", y_down, down, up), ("ad", y_up, up, down))[m]
        there = held.at[m, c, rows(k, b)]
        arrived(f"{name}{k}{m}", there, source)
        send(f"f{k}{m}", there, there, peer)
        send(f"fc{k}{m}", there, there, other)

    def H(k, m):
        name, b, source = (("ad", y_up, up), ("au", y_down, down))[m]
        there = held.at[m, c, rows(k, b)]
        arrived(f"{name}{k}{m}", there, source)
        send(f"hc{k}{m}", there, there, other)

    def E(k, m):
        far = held.at[m, c, rows(k, y_far)]
        arrived(f"f{k}{m}", far, (down, up)[m])
        send(f"ec{k}{m}", far, far, other)

    def whole(k, m):
        arrived(f"ac{k}{m}", held.at[m, oc, rows(k, y)], other)
        arrived(f"fc{k}{m}", held.at[m, oc, rows(k, (y_down, y_up)[m])], other)
        arrived(f"hc{k}{m}", held.at[m, oc, rows(k, (y_up, y_down)[m])], other)
        arrived(f"ec{k}{m}", held.at[m, oc, rows(k, y_far)], other)

    def I(k):
        whole(k, 1)
        at = slice(k * CHUNK, (k + 1) * CHUNK)
        partial[k] = nt(held[1, 0, at, :], w_up[:, :HALF]) + nt(held[1, 1, at, :], w_up[:, HALF:])
        if k == 3:
            last[...] = partial[k].astype(BF16)
        for d in (1, 0, 2):
            if k == 3:
                send(f"ix{k}{d}", last.at[block(xs[d])], x_last.at[d], x_peers[d])
            else:
                send(f"ix{k}{d}", partial.at[k, block(xs[d])], x_in.at[k, d], x_peers[d])

    def J(k):
        landed = x_last if k == 3 else x_in.at[k]
        for d in range(3):
            arrived(f"ix{k}{d}", landed.at[d], x_peers[d])
        summed = partial[k, block(x), :]
        for d in range(3):
            summed = summed + landed[d].astype(F32)
        if k == 0:
            partial[k, block(x), :] = summed
        elif k == 3:
            iz_out_last[...] = summed.astype(BF16)
            send(f"iz{k}", iz_out_last, iz_in_last, plane_peers[k])
        else:
            iz_out[k - 1] = summed
            send(f"iz{k}", iz_out.at[k - 1], iz_in.at[k - 1], plane_peers[k])

    stores = []

    def store(src, dst):
        copy = pltpu.make_async_copy(src, dst, store_sem.at[len(stores)])
        copy.start()
        stores.append(copy)

    def T():
        for m in range(2):
            acts_t[m] = acts[m].T

    def G(m):
        out = (down_out, up_out)[m]
        if m == 0:
            for k in range(4):
                whole(k, 0)
        for h in range(2):
            at = pl.ds(h * HALF, HALF)
            out[:, at] = jnp.dot(acts_t[1 - m], held[m, h], preferred_element_type=F32).astype(BF16)

    stages = dict(P=P, U=U, C=C, R=R, Z=Z, A=A, F=F, H=H, E=E, I=I, J=J, T=T, G=G)
    for item in ORDER:
        stages[item[0]](*map(int, item[1:]))

    for copy in sends[:-4]:
        copy.wait_send()
    summed = partial[0, block(x), :]
    for k in (1, 2):
        arrived(f"iz{k}", iz_in.at[k - 1], plane_peers[k])
        summed = summed + iz_in[k - 1]
    arrived("iz3", iz_in_last, plane_peers[3])
    summed = summed + iz_in_last[...].astype(F32)
    ig_out[...] = summed.astype(BF16)
    store(ig_out, ig_hbm)
    for copy in sends[-4:]:
        copy.wait_send()
    for copy in stores:
        copy.wait()


def hand_over(ig, up, down, ig_to, up_to, down_to, sem):
    pairs = ((up, up_to), (down, down_to), (ig, ig_to))
    copies = [pltpu.make_async_copy(a, b, sem.at[i]) for i, (a, b) in enumerate(pairs)]
    for copy in copies:
        copy.start()
    for copy in copies:
        copy.wait()


def shards(inputs, out_grad, w_up, w_down):
    anywhere = pl.BlockSpec(memory_space=pl.ANY)
    n = len(NAMES)
    input_grad, up_grad, down_grad_t = pl.pallas_call(
        kernel,
        out_shape=(
            jax.ShapeDtypeStruct((BLOCK, FEATS), BF16),
            jax.ShapeDtypeStruct((FEATS, 2 * HALF), BF16),
            jax.ShapeDtypeStruct((FEATS, 2 * HALF), BF16),
        ),
        in_specs=[pl.BlockSpec(memory_space=pltpu.HBM)] * 4,
        out_specs=(anywhere,) + (pl.BlockSpec(memory_space=pltpu.VMEM),) * 2,
        scratch_shapes=[
            pltpu.VMEM((2, PLANES * CHUNK, FEATS), BF16),
            pltpu.VMEM((FEATS, 2 * HALF), BF16),
            pltpu.VMEM((FEATS, 2 * HALF), BF16),
            pltpu.VMEM((PLANES, 2, CHUNK, HALF), F32),
            pltpu.VMEM((PLANES, 2, CHUNK, HALF), F32),
            pltpu.VMEM((PLANES, 2, CHUNK, HALF), F32),
            pltpu.VMEM((PLANES, 2, CHUNK, HALF), BF16),
            pltpu.VMEM((PLANES, 2, BLOCK, HALF), BF16),
            pltpu.VMEM((PLANES, 2, BLOCK, HALF), BF16),
            pltpu.VMEM((PLANES, 2, BLOCK, HALF), BF16),
            pltpu.VMEM((PLANES, 2, BLOCK, HALF), F32),
            pltpu.VMEM((PLANES, 2, BLOCK, HALF), BF16),
            pltpu.VMEM((PLANES, 2, BLOCK, HALF), BF16),
            pltpu.VMEM((2, 2, PLANES * CHUNK, HALF), BF16),
            pltpu.VMEM((PLANES, CHUNK, FEATS), F32),
            pltpu.VMEM((3, 3, BLOCK, FEATS), F32),
            pltpu.VMEM((2, BLOCK, FEATS), F32),
            pltpu.VMEM((2, BLOCK, FEATS), F32),
            pltpu.VMEM((CHUNK, FEATS), BF16),
            pltpu.VMEM((3, BLOCK, FEATS), BF16),
            pltpu.VMEM((BLOCK, FEATS), BF16),
            pltpu.VMEM((BLOCK, FEATS), BF16),
            pltpu.VMEM((BLOCK, FEATS), BF16),
            pltpu.VMEM((2, FEATS, PLANES * CHUNK), BF16),
            pltpu.SemaphoreType.DMA((4,)),
            pltpu.SemaphoreType.DMA((1,)),
            pltpu.SemaphoreType.DMA((n,)),
            pltpu.SemaphoreType.DMA((n,)),
        ],
        compiler_params=pltpu.CompilerParams(collective_id=0, has_side_effects=True, vmem_limit_bytes=46 * 2**20),
        cost_estimate=pl.CostEstimate(flops=6_800_000_000, bytes_accessed=11_000_000, transcendentals=0),
        name="ffn_backward",
    )(*(pltpu.with_memory_space_constraint(a, pltpu.HBM) for a in (inputs, out_grad, w_up, w_down.T)))
    input_grad, up_grad, down_grad_t = pl.pallas_call(
        hand_over,
        out_shape=tuple(jax.ShapeDtypeStruct(a.shape, a.dtype) for a in (input_grad, up_grad, down_grad_t)),
        in_specs=[anywhere] * 3,
        out_specs=(anywhere,) * 3,
        scratch_shapes=[pltpu.SemaphoreType.DMA((3,))],
        compiler_params=pltpu.CompilerParams(vmem_limit_bytes=2 * 2**20),
        cost_estimate=pl.CostEstimate(flops=0, bytes_accessed=10_700_000, transcendentals=0),
        name="hand_over",
    )(input_grad, up_grad, down_grad_t)
    return input_grad, up_grad, down_grad_t.T


def solution(mesh):
    in_specs = (P("col", "row"), P("col", "row"), P("row", "col"), P("col", "row"))
    out_specs = (P("col", "row"), P("row", "col"), P("col", "row"))
    return jax.shard_map(shards, mesh=mesh, in_specs=in_specs, out_specs=out_specs, check_vma=False)
```
